32 devices in a mesh: row: 8 (over y, x, core), col: 4 (over z).
Axes of the slice: x: 2, y: 2, z: 4, core: 2. Of those that a mesh axis runs over, the one named last changes fastest.
Arguments:
- noise: float32 [512, 36, 1024], P('col', None, 'row'), may hold values from -6 to 6
- factor: bfloat16 [31, 1024, 3, 5120], P(None, 'row', None, 'col'), may hold values from -0.0390625 to 0.0390625
- dinv: bfloat16 [3, 5120, 5, 1024], P(None, 'col', None, 'row'), as said below
Outputs:
- solved: bfloat16 [3, 5120, 512], P(None, 'col')
- remaining: float32 [512, 36, 1024], P('col', None, 'row')
The draws below stay inside these ranges and needn't reach their ends.
Inputs may be any that keep to these rules, and one draw needn't show every extreme that they name: dinv[s], read as a 5120 x 5120 matrix, is lower triangular with a positive diagonal.
All inputs are finite; a program needn't handle non-finite values.
Results may differ from the reference program's by a relative error of at most 0.007.
Values may be sent and summed in bfloat16 or wider, within the bound.
A program may use at most 128 MiB of HBM per device.

```python
import jax
import jax.numpy as jnp
from jax import lax

N = 36864
RHS = 512
RB = 128
STEPS = 3
PW = 5120
DR = 5
RBLK = 36
N_ROW = 8


def draw_dinv(key, part):
    key_off, key_diag = jax.random.split(jax.random.fold_in(key, 17))
    shape = (STEPS, PW, DR, N_ROW * RB)
    row_ids = lax.broadcasted_iota(jnp.int32, shape, 1)
    col_ids = lax.broadcasted_iota(jnp.int32, shape, 2) * (N_ROW * RB) + lax.broadcasted_iota(jnp.int32, shape, 3)
    offdiag = jax.random.normal(key_off, shape, jnp.float32)
    offdiag = offdiag * jnp.float32(PW) ** (-0.5)
    diagonal = jax.random.uniform(key_diag, shape, jnp.float32, 0.5, 1.5)
    values = jnp.where(col_ids < row_ids, offdiag, 0.0) + jnp.where(col_ids == row_ids, diagonal, 0.0)
    return values.astype(jnp.bfloat16)


def levels(key, extent, pieces, least, top_value):
    gain, own = 1.0, jax.random.fold_in(key, 6)
    for dim, shards_of in pieces:
        heights = jnp.exp(jax.random.uniform(jax.random.fold_in(own, dim), (shards_of,), jnp.float32, least / len(pieces), top_value / len(pieces)))
        gain = gain * jnp.repeat(heights, extent[dim] // shards_of).reshape([-1 if axis == dim else 1 for axis in range(len(extent))])
    return gain


def normal_values(own_key, shape, scale, reach, shards=(), kind=jnp.bfloat16):
    values = jax.random.normal(own_key, shape, jnp.float32) * scale
    if len(shards) > 0:
        values = levels(own_key, shape, shards, -0.22, 0.18) * values
    return jnp.clip(values, min=-reach, max=reach).astype(kind)


def setup_inputs(seed: int = 0) -> dict:
    key_of = jax.random.split(jax.random.key(seed), 4)
    return {
        "noise": normal_values(key_of[0], (RHS, RBLK, N_ROW * RB), 1.0, 6.0, ((0, 4), (2, 8)), jnp.float32),
        "factor": normal_values(key_of[1], (RBLK - DR, N_ROW * RB, STEPS, PW), (4 * PW) ** -0.5, 0.0390625, ((1, 8), (3, 4))),
        "dinv": draw_dinv(jax.random.fold_in(key_of[3], 71), 0),
    }


def reference(noise, factor, dinv):
    width = PW
    work = noise.reshape(RHS, N).astype(jnp.float32)
    solved_list = []
    for step_idx in range(STEPS):
        current = work[:, step_idx * width:(step_idx + 1) * width].astype(jnp.bfloat16)
        inverse = dinv[step_idx].reshape(width, width).astype(jnp.float32)
        solution = jnp.dot(inverse, current.astype(jnp.float32).T, precision=lax.Precision.HIGHEST).astype(jnp.bfloat16)
        solved_list.append(solution)
        panel_rows = factor[:, :, step_idx, :].reshape((RBLK - DR) * N_ROW * RB, width)[step_idx * width:]
        update = jnp.dot(panel_rows.astype(jnp.float32), solution.astype(jnp.float32), precision=lax.Precision.HIGHEST)
        work = work.at[:, (step_idx + 1) * width:].add(-update.T)
    remaining = work.reshape(RHS, RBLK, N_ROW * RB)
    return jnp.stack(solved_list), remaining
```

```python
import jax
import jax.numpy as jnp
from jax import lax
from jax.sharding import PartitionSpec as P

BF16 = jnp.bfloat16
F32 = jnp.float32


def local(noise, factor, dinv):
    steps = dinv.shape[0]
    rounds = dinv.shape[2]
    work = jnp.transpose(noise, (1, 0, 2))
    rows = jnp.transpose(factor, (2, 0, 1, 3))
    blocks = jnp.transpose(dinv, (0, 2, 1, 3))
    solved = []
    done = []
    for s in range(steps):
        current = work[s * rounds : (s + 1) * rounds]
        if s > 0:
            update = sum(
                jnp.einsum("apq,qh->ahp", rows[t, (s - 1) * rounds : s * rounds], solved[t], preferred_element_type=F32)
                for t in range(s)
            )
            current = current - lax.psum_scatter(update.astype(BF16), "col", scatter_dimension=1, tiled=True).astype(F32)
        done.append(current)
        gathered = lax.all_gather(current.astype(BF16), "col", axis=1, tiled=True)
        partial_sum = jnp.einsum("dqp,dhp->qh", blocks[s], gathered, preferred_element_type=F32)
        solved.append(lax.psum(partial_sum.astype(BF16), "row"))
    update = sum(
        jnp.einsum("apq,qh->ahp", rows[t, (steps - 1) * rounds :], solved[t], preferred_element_type=F32)
        for t in range(steps)
    )
    last = work[steps * rounds :] - lax.psum_scatter(update.astype(BF16), "col", scatter_dimension=1, tiled=True).astype(F32)
    done.append(last)
    remaining = jnp.transpose(jnp.concatenate(done, axis=0), (1, 0, 2))
    return jnp.stack(solved), remaining


def solution(mesh):
    placed = (P("col", None, "row"), P(None, "row", None, "col"), P(None, "col", None, "row"))
    return jax.shard_map(
        local,
        mesh=mesh,
        in_specs=placed,
        out_specs=(P(None, "col", None), P("col", None, "row")),
        check_vma=False,
    )
```

```python
import functools

import jax
import jax.numpy as jnp
from jax import lax
from jax.experimental import pallas as pl
from jax.experimental.pallas import tpu as pltpu
from jax.sharding import PartitionSpec as P

BF16 = jnp.bfloat16
F32 = jnp.float32
CHAINS = 2
SLOTS = 3
QB = 256


def dot_t(a, b):
    return lax.dot_general(a, b, (((1,), (1,)), ((), ())), preferred_element_type=F32)


def remote(src, dst, send_sem, recv_sem, axis, index):
    return pltpu.make_async_remote_copy(
        src_ref=src,
        dst_ref=dst,
        send_sem=send_sem,
        recv_sem=recv_sem,
        device_id={axis: index},
        device_id_type=pl.DeviceIdType.MESH,
    )


def kernel(
    nr, nc, noise, factor, dinv, out_solved, out_rest,
    dv, lp, lf, st, cur, wsum, rsend, rrecv, pz, zsend, zrecv, pf, frecv,
    dv_sem, lp_sem, lf_sem, out_sem,
    g_ss, g_rs, r_ss, r_rs, z_ss, z_rs, f_ss, f_rs,
):
    steps, rounds, width = dv.shape[0], dv.shape[1], dv.shape[2]
    hl = noise.shape[1]
    hc = hl // CHAINS
    rows = nc * hc
    groups, gs = pf.shape[0], lf.shape[2]
    bits = nr.bit_length() - 1
    first = (steps - 1) * rounds
    r = lax.axis_index("row")
    c = lax.axis_index("col")
    right = jnp.minimum(c + 1, nc - 1)
    left = jnp.maximum(c - 1, 0)
    has_left = c > 0
    has_right = c < nc - 1

    def partner(b):
        return r + (1 - 2 * ((r // (1 << b)) % 2)) * (1 << b)

    dv_copy = [pltpu.make_async_copy(dinv.at[s], dv.at[s], dv_sem.at[s]) for s in range(steps)]
    pairs = [(s, t) for s in range(1, steps) for t in range(s)]
    lp_copy = [
        pltpu.make_async_copy(factor.at[pl.ds((s - 1) * rounds, rounds), t], lp.at[i], lp_sem.at[i])
        for i, (s, t) in enumerate(pairs)
    ]

    def lf_copy(group, t):
        slot = lax.rem(group, SLOTS)
        return pltpu.make_async_copy(
            factor.at[pl.ds(first + group * gs, gs), t], lf.at[slot, t], lf_sem.at[slot, t]
        )

    for copy in dv_copy + lp_copy:
        copy.start()
    for group in range(min(SLOTS, groups)):
        for t in range(steps):
            lf_copy(group, t).start()

    barrier = pltpu.get_barrier_semaphore()
    for b in range(bits):
        pl.semaphore_signal(
            barrier, inc=1, device_id={"row": partner(b)}, device_id_type=pl.DeviceIdType.MESH
        )

    @pl.when(has_left)
    def _():
        pl.semaphore_signal(barrier, inc=1, device_id={"col": left}, device_id_type=pl.DeviceIdType.MESH)

    @pl.when(has_right)
    def _():
        pl.semaphore_signal(barrier, inc=1, device_id={"col": right}, device_id_type=pl.DeviceIdType.MESH)

    pl.semaphore_wait(barrier, bits + has_left.astype(jnp.int32) + has_right.astype(jnp.int32))

    ready = set()

    def need(key, copy):
        if key not in ready:
            ready.add(key)
            copy.wait()

    def own_rows():
        return pl.ds(pl.multiple_of(c * hc, 16), hc)

    def gather(k):
        cur[k, :, own_rows(), :] = noise[0:rounds, k * hc : (k + 1) * hc, :].astype(BF16)

        def chunk(j, d, t, to):
            ref = cur.at[k, :, pl.ds(pl.multiple_of(j * hc, 16), hc), :]
            return remote(ref, ref, g_ss.at[k, d, t], g_rs.at[k, d, t], "col", to)

        for t in range(nc - 1):

            @pl.when(has_right & (c >= t))
            def _():
                chunk(c - t, 0, t, right).start()

            @pl.when(has_left & (c + t < nc))
            def _():
                chunk(c + t, 1, t, left).start()

            yield

            @pl.when(c - 1 - t >= 0)
            def _():
                chunk(c - 1 - t, 0, t, right).wait_recv()

            @pl.when(c + 1 + t < nc)
            def _():
                chunk(c + 1 + t, 1, t, left).wait_recv()

        for t in range(nc - 1):

            @pl.when(has_right & (c >= t))
            def _():
                chunk(c - t, 0, t, right).wait_send()

            @pl.when(has_left & (c + t < nc))
            def _():
                chunk(c + t, 1, t, left).wait_send()

    def inverse(s, k):
        need(("dv", s), dv_copy[s])
        lhs = jnp.concatenate([cur[k, d] for d in range(rounds)], axis=-1)

        @pl.loop(0, width // QB)
        def _(i):
            q = pl.ds(pl.multiple_of(i * QB, QB), QB)
            rhs = jnp.concatenate([dv[s, d, q, :] for d in range(rounds)], axis=-1)
            wsum[k, :, q] = dot_t(lhs, rhs)

    def rowsum(s, k):
        order = list(range(bits))
        if k % 2 == 1:
            order = order[:1] + order[1:][::-1]
        base = jnp.int32(0)
        size = rows
        place = 0
        for i, b in enumerate(order):
            half = size // 2
            bit = (r // (1 << b)) % 2
            keep = pl.multiple_of(base + bit * half, 16)
            away = pl.multiple_of(base + (1 - bit) * half, 16)
            area = pl.ds(place, half)
            rsend[k, area, :] = wsum[k, pl.ds(away, half), :].astype(BF16)
            copy = remote(
                rsend.at[k, area], rrecv.at[s, k, area], r_ss.at[s, k, i], r_rs.at[s, k, i], "row", partner(b)
            )
            copy.start()
            yield
            copy.wait_recv()
            total = wsum[k, pl.ds(keep, half), :] + rrecv[s, k, area, :].astype(F32)
            if i < bits - 1:
                wsum[k, pl.ds(keep, half), :] = total
            else:
                st[s, k, pl.ds(keep, half), :] = total.astype(BF16)
            copy.wait_send()
            base, size = keep, half
            place += half
        for i, b in reversed(list(enumerate(order))):
            bit = (r // (1 << b)) % 2
            mine = st.at[s, k, pl.ds(pl.multiple_of(base, 16), size)]
            j = bits + i
            copy = remote(mine, mine, r_ss.at[s, k, j], r_rs.at[s, k, j], "row", partner(b))
            copy.start()
            yield
            copy.wait()
            base = base - bit * size
            size = size * 2
        for j in range(nc):
            pltpu.make_async_copy(
                st.at[s, k, pl.ds(j * hc, hc)],
                out_solved.at[s, j, pl.ds(k * hc, hc)],
                out_sem.at[s, k, j],
            ).start()

    def colsum(s, k):
        mine = [(i, t) for i, (s_, t) in enumerate(pairs) if s_ == s]
        for i, _ in mine:
            need(("lp", i), lp_copy[i])

        @pl.loop(0, rounds)
        def _(a):
            pz[k, a] = -sum(dot_t(st[t, k], lp[i, a]) for i, t in mine)
            pz[k, a, own_rows(), :] += noise[s * rounds + a, k * hc : (k + 1) * hc, :]

        def message(a, d, to):
            return remote(
                zsend.at[k, d, a], zrecv.at[s - 1, k, d, a], z_ss.at[s - 1, k, d, a], z_rs.at[s - 1, k, d, a], "col", to
            )

        def move(a, d, receives, sends, to):
            @pl.when((a >= 0) & (a < rounds))
            def _():
                @pl.when(receives)
                def _():
                    message(a, d, to).wait_recv()

                @pl.when(sends & receives)
                def _():
                    zsend[k, d, a] = (pz[k, a] + zrecv[s - 1, k, d, a].astype(F32)).astype(BF16)

                @pl.when(sends & jnp.logical_not(receives))
                def _():
                    zsend[k, d, a] = pz[k, a].astype(BF16)

                @pl.when(sends)
                def _():
                    message(a, d, to).start()

        for tau in range(rounds + nc - 1):
            move(tau - c, 0, has_left, has_right, right)
            move(tau - (nc - 1 - c), 1, has_right, has_left, left)
            yield

        @pl.loop(0, rounds)
        def _(a):
            @pl.when(has_left)
            def _():
                pz[k, a] += zrecv[s - 1, k, 0, a].astype(F32)

            @pl.when(has_right)
            def _():
                pz[k, a] += zrecv[s - 1, k, 1, a].astype(F32)

            cur[k, a] = pz[k, a].astype(BF16)
            out_rest[s * rounds + a, k * hc : (k + 1) * hc, :] = pz[k, a, own_rows(), :]

            @pl.when(has_right)
            def _():
                message(a, 0, right).wait_send()

            @pl.when(has_left)
            def _():
                message(a, 1, left).wait_send()

    def chain(k):
        yield from gather(k)
        for s in range(steps):
            inverse(s, k)
            yield from rowsum(s, k)
            if s < steps - 1:
                yield from colsum(s + 1, k)

    live = [chain(k) for k in range(CHAINS)]
    while live:
        for one in list(live):
            if next(one, live) is live:
                live.remove(one)

    out_rest[0:rounds] = noise[0:rounds]

    def part(g, d, j, to):
        ref = frecv.at[d, g, j]
        return remote(ref, ref, f_ss.at[d, g, j], f_rs.at[d, g, j], "col", to)

    def pass_on(g, d, receives, lo, hi, to):
        @pl.when((g >= 0) & (g < groups))
        def _():
            @pl.when(receives)
            def _():
                part(g, d, c, to).wait_recv()

            def one(i, _):
                j = (hi - 1 - i) if d == 0 else (lo + i)

                @pl.when(receives)
                def _():
                    part(g, d, j, to).wait_recv()
                    frecv[d, g, j] = (pf[g, :, j] + frecv[d, g, j].astype(F32)).astype(BF16)

                @pl.when(jnp.logical_not(receives))
                def _():
                    frecv[d, g, j] = pf[g, :, j].astype(BF16)

                part(g, d, j, to).start()
                return 0

            lax.fori_loop(0, hi - lo, one, 0)

    lag = jnp.maximum(c, nc - 1 - c)

    def turn(tau, _):
        @pl.when(tau < groups)
        def _():
            for t in range(steps):
                lf_copy(tau, t).wait()
            slot = lax.rem(tau, SLOTS)
            for k in range(CHAINS):
                acc = sum(dot_t(st[t, k], lf[slot, t].reshape(gs * 128, width)) for t in range(steps))
                pf[tau, k] = -acc.reshape(nc, hc, gs * 128)

            @pl.when(tau + SLOTS < groups)
            def _():
                for t in range(steps):
                    lf_copy(tau + SLOTS, t).start()

        pass_on(tau - c, 0, has_left, c + 1, nc, right)
        pass_on(tau - (nc - 1 - c), 1, has_right, 0, c, left)
        g = tau - lag

        @pl.when((g >= 0) & (g < groups))
        def _():
            @pl.when(has_left)
            def _():
                pf[g, :, c] += frecv[0, g, c].astype(F32)

            @pl.when(has_right)
            def _():
                pf[g, :, c] += frecv[1, g, c].astype(F32)

            for i in range(gs):
                a = steps * rounds + g * gs + i
                total = pf[g, :, c, :, i * 128 : (i + 1) * 128].reshape(hl, 128)
                out_rest[a] = noise[a] + total

        return 0

    lax.fori_loop(0, groups + nc - 1, turn, 0)

    def finish(g, _):
        def sent(d, to):
            def one(j, _):
                part(g, d, j, to).wait_send()
                return 0

            return one

        lax.fori_loop(c + 1, nc, sent(0, right), 0)
        lax.fori_loop(0, c, sent(1, left), 0)
        return 0

    lax.fori_loop(0, groups, finish, 0)
    for s in range(steps):
        for k in range(CHAINS):
            for j in range(nc):
                pltpu.make_async_copy(
                    st.at[s, k, pl.ds(j * hc, hc)],
                    out_solved.at[s, j, pl.ds(k * hc, hc)],
                    out_sem.at[s, k, j],
                ).wait()


def local(nr, nc, noise, factor, dinv):
    hl, rblk, rb = noise.shape
    steps, width, rounds, _ = dinv.shape
    below = factor.shape[0] - (steps - 1) * rounds
    gs = next(x for x in (3, 2, 1) if below % x == 0)
    groups = below // gs
    hc = hl // CHAINS
    rows = nc * hc
    bits = nr.bit_length() - 1
    vm = pltpu.VMEM
    dma = pltpu.SemaphoreType.DMA
    npairs = steps * (steps - 1) // 2
    solved, rest = pl.pallas_call(
        functools.partial(kernel, nr, nc),
        out_shape=(
            jax.ShapeDtypeStruct((steps, nc, hl, width), BF16),
            jax.ShapeDtypeStruct((rblk, hl, rb), F32),
        ),
        in_specs=[
            pl.BlockSpec(memory_space=pltpu.VMEM),
            pl.BlockSpec(memory_space=pl.ANY),
            pl.BlockSpec(memory_space=pl.ANY),
        ],
        out_specs=(pl.BlockSpec(memory_space=pl.ANY), pl.BlockSpec(memory_space=pltpu.VMEM)),
        scratch_shapes=[
            vm((steps, rounds, width, rb), BF16),
            vm((npairs, rounds, rb, width), BF16),
            vm((SLOTS, steps, gs, rb, width), BF16),
            vm((steps, CHAINS, rows, width), BF16),
            vm((CHAINS, rounds, rows, rb), BF16),
            vm((CHAINS, rows, width), F32),
            vm((CHAINS, rows, width), BF16),
            vm((steps, CHAINS, rows, width), BF16),
            vm((CHAINS, rounds, rows, rb), F32),
            vm((CHAINS, 2, rounds, rows, rb), BF16),
            vm((steps - 1, CHAINS, 2, rounds, rows, rb), BF16),
            vm((groups, CHAINS, nc, hc, gs * rb), F32),
            vm((2, groups, nc, CHAINS, hc, gs * rb), BF16),
            dma((steps,)),
            dma((npairs,)),
            dma((SLOTS, steps)),
            dma((steps, CHAINS, nc)),
            dma((CHAINS, 2, nc)),
            dma((CHAINS, 2, nc)),
            dma((steps, CHAINS, 2 * bits)),
            dma((steps, CHAINS, 2 * bits)),
            dma((steps - 1, CHAINS, 2, rounds)),
            dma((steps - 1, CHAINS, 2, rounds)),
            dma((2, groups, nc)),
            dma((2, groups, nc)),
        ],
        compiler_params=pltpu.CompilerParams(
            collective_id=0, has_side_effects=True, vmem_limit_bytes=60 * 1024 * 1024
        ),
    )(
        jnp.transpose(noise, (1, 0, 2)),
        jnp.transpose(factor, (0, 2, 1, 3)),
        jnp.transpose(dinv, (0, 2, 1, 3)),
    )
    solved = jnp.transpose(solved.reshape(steps, nc * hl, width), (0, 2, 1))
    return solved, jnp.transpose(rest, (1, 0, 2))


def solution(mesh):
    placed = (P("col", None, "row"), P(None, "row", None, "col"), P(None, "col", None, "row"))
    return jax.shard_map(
        functools.partial(local, mesh.shape["row"], mesh.shape["col"]),
        mesh=mesh,
        in_specs=placed,
        out_specs=(P(None, "col", None), P("col", None, "row")),
        check_vma=False,
    )
```

```python
import functools

import jax
import jax.numpy as jnp
from jax import lax
from jax.experimental import pallas as pl
from jax.experimental.pallas import tpu as pltpu
from jax.sharding import PartitionSpec as P

BF16 = jnp.bfloat16
F32 = jnp.float32
CHAINS = 2
SLOTS = 2
LAG = 7
QB = 256


def dot_t(a, b):
    return lax.dot_general(a, b, (((1,), (1,)), ((), ())), preferred_element_type=F32)


def remote(src, dst, send_sem, recv_sem, axis, index):
    return pltpu.make_async_remote_copy(
        src_ref=src,
        dst_ref=dst,
        send_sem=send_sem,
        recv_sem=recv_sem,
        device_id={axis: index},
        device_id_type=pl.DeviceIdType.MESH,
    )


def kernel(
    nr, nc, noise, factor, dinv, out_solved, out_rest,
    dv, lp, lf, st, cur, wsum, rsend, rrecv, pz, zsend, zrecv, pf, frecv,
    dv_sem, lp_sem, lf_sem,
    g_ss, g_rs, r_ss, r_rs, z_ss, z_rs, f_ss, f_rs,
):
    steps, rounds, width = dv.shape[0], dv.shape[1], dv.shape[2]
    hl = noise.shape[1]
    hc = hl // CHAINS
    rows = nc * hc
    groups, gs = pf.shape[0], lf.shape[3]
    bits = nr.bit_length() - 1
    first = (steps - 1) * rounds
    r = lax.axis_index("row")
    c = lax.axis_index("col")
    right = jnp.minimum(c + 1, nc - 1)
    left = jnp.maximum(c - 1, 0)
    has_left = c > 0
    has_right = c < nc - 1

    def partner(b):
        return r + (1 - 2 * ((r // (1 << b)) % 2)) * (1 << b)

    dv_copy = [pltpu.make_async_copy(dinv.at[s], dv.at[s], dv_sem.at[s]) for s in range(steps)]
    pairs = [(s, t) for s in range(1, steps) for t in range(s)]
    lp_copy = [
        pltpu.make_async_copy(factor.at[pl.ds((s - 1) * rounds, rounds), t], lp.at[i], lp_sem.at[i])
        for i, (s, t) in enumerate(pairs)
    ]

    def lf_copy(k, group, t):
        slot = lax.rem(group, SLOTS)
        return pltpu.make_async_copy(
            factor.at[pl.ds(first + group * gs, gs), t], lf.at[k, slot, t], lf_sem.at[k, slot, t]
        )

    for copy in dv_copy + lp_copy:
        copy.start()
    for k in range(CHAINS):
        for group in range(min(SLOTS, groups)):
            for t in range(steps):
                lf_copy(k, jnp.int32(group), t).start()

    barrier = pltpu.get_barrier_semaphore()
    for b in range(bits):
        pl.semaphore_signal(
            barrier, inc=1, device_id={"row": partner(b)}, device_id_type=pl.DeviceIdType.MESH
        )

    @pl.when(has_left)
    def _():
        pl.semaphore_signal(barrier, inc=1, device_id={"col": left}, device_id_type=pl.DeviceIdType.MESH)

    @pl.when(has_right)
    def _():
        pl.semaphore_signal(barrier, inc=1, device_id={"col": right}, device_id_type=pl.DeviceIdType.MESH)

    pl.semaphore_wait(barrier, bits + has_left.astype(jnp.int32) + has_right.astype(jnp.int32))

    ready = set()

    def need(key, copy):
        if key not in ready:
            ready.add(key)
            copy.wait()

    def own_rows():
        return pl.ds(pl.multiple_of(c * hc, 16), hc)

    def gather(k):
        cur[k, :, own_rows(), :] = noise[0:rounds, k * hc : (k + 1) * hc, :].astype(BF16)

        def chunk(j, d, t, to):
            ref = cur.at[k, :, pl.ds(pl.multiple_of(j * hc, 16), hc), :]
            return remote(ref, ref, g_ss.at[k, d, t], g_rs.at[k, d, t], "col", to)

        for t in range(nc - 1):

            @pl.when(has_right & (c >= t))
            def _():
                chunk(c - t, 0, t, right).start()

            @pl.when(has_left & (c + t < nc))
            def _():
                chunk(c + t, 1, t, left).start()

            yield

            @pl.when(c - 1 - t >= 0)
            def _():
                chunk(c - 1 - t, 0, t, right).wait_recv()

            @pl.when(c + 1 + t < nc)
            def _():
                chunk(c + 1 + t, 1, t, left).wait_recv()

        for t in range(nc - 1):

            @pl.when(has_right & (c >= t))
            def _():
                chunk(c - t, 0, t, right).wait_send()

            @pl.when(has_left & (c + t < nc))
            def _():
                chunk(c + t, 1, t, left).wait_send()

    def inverse(s, k):
        need(("dv", s), dv_copy[s])
        lhs = jnp.concatenate([cur[k, d] for d in range(rounds)], axis=-1)

        @pl.loop(0, width // QB)
        def _(i):
            q = pl.ds(pl.multiple_of(i * QB, QB), QB)
            rhs = jnp.concatenate([dv[s, d, q, :] for d in range(rounds)], axis=-1)
            wsum[k, :, q] = dot_t(lhs, rhs)

    def rowsum(s, k):
        order = list(range(bits))
        if k % 2 == 1:
            order = order[:1] + order[1:][::-1]
        base = jnp.int32(0)
        size = rows
        place = 0
        for i, b in enumerate(order):
            half = size // 2
            bit = (r // (1 << b)) % 2
            keep = pl.multiple_of(base + bit * half, 16)
            away = pl.multiple_of(base + (1 - bit) * half, 16)
            area = pl.ds(place, half)
            rsend[k, area, :] = wsum[k, pl.ds(away, half), :].astype(BF16)
            copy = remote(
                rsend.at[k, area], rrecv.at[s, k, area], r_ss.at[s, k, i], r_rs.at[s, k, i], "row", partner(b)
            )
            copy.start()
            yield
            copy.wait_recv()
            total = wsum[k, pl.ds(keep, half), :] + rrecv[s, k, area, :].astype(F32)
            if i < bits - 1:
                wsum[k, pl.ds(keep, half), :] = total
            else:
                st[s, k, pl.ds(keep, half), :] = total.astype(BF16)
            copy.wait_send()
            base, size = keep, half
            place += half
        for i, b in reversed(list(enumerate(order))):
            bit = (r // (1 << b)) % 2
            mine = st.at[s, k, pl.ds(pl.multiple_of(base, 16), size)]
            j = bits + i
            copy = remote(mine, mine, r_ss.at[s, k, j], r_rs.at[s, k, j], "row", partner(b))
            copy.start()
            yield
            copy.wait()
            base = base - bit * size
            size = size * 2

    def colsum(s, k):
        mine = [(i, t) for i, (s_, t) in enumerate(pairs) if s_ == s]
        for i, _ in mine:
            need(("lp", i), lp_copy[i])

        @pl.loop(0, rounds)
        def _(a):
            pz[k, a] = -sum(dot_t(st[t, k], lp[i, a]) for i, t in mine)
            pz[k, a, own_rows(), :] += noise[s * rounds + a, k * hc : (k + 1) * hc, :]

        def message(a, d, to):
            return remote(
                zsend.at[k, d, a], zrecv.at[s - 1, k, d, a], z_ss.at[s - 1, k, d, a], z_rs.at[s - 1, k, d, a], "col", to
            )

        def move(a, d, receives, sends, to):
            @pl.when((a >= 0) & (a < rounds))
            def _():
                @pl.when(receives)
                def _():
                    message(a, d, to).wait_recv()

                @pl.when(sends & receives)
                def _():
                    zsend[k, d, a] = (pz[k, a] + zrecv[s - 1, k, d, a].astype(F32)).astype(BF16)

                @pl.when(sends & jnp.logical_not(receives))
                def _():
                    zsend[k, d, a] = pz[k, a].astype(BF16)

                @pl.when(sends)
                def _():
                    message(a, d, to).start()

        for tau in range(rounds + nc - 1):
            move(tau - c, 0, has_left, has_right, right)
            move(tau - (nc - 1 - c), 1, has_right, has_left, left)
            yield

        @pl.loop(0, rounds)
        def _(a):
            @pl.when(has_left)
            def _():
                pz[k, a] += zrecv[s - 1, k, 0, a].astype(F32)

            @pl.when(has_right)
            def _():
                pz[k, a] += zrecv[s - 1, k, 1, a].astype(F32)

            cur[k, a] = pz[k, a].astype(BF16)
            out_rest[s * rounds + a, k * hc : (k + 1) * hc, :] = pz[k, a, own_rows(), :]

            @pl.when(has_right)
            def _():
                message(a, 0, right).wait_send()

            @pl.when(has_left)
            def _():
                message(a, 1, left).wait_send()

    def part(k, g, d, j, to):
        ref = frecv.at[d, g, k, j]
        return remote(ref, ref, f_ss.at[d, g, k, j], f_rs.at[d, g, k, j], "col", to)

    def pass_on(k, g, d, receives, lo, hi, to):
        @pl.when((g >= 0) & (g < groups))
        def _():
            def one(i, _):
                j = (hi - 1 - i) if d == 0 else (lo + i)

                @pl.when(receives)
                def _():
                    part(k, g, d, j, to).wait_recv()
                    frecv[d, g, k, j] = (pf[g, k, j] + frecv[d, g, k, j].astype(F32)).astype(BF16)

                @pl.when(jnp.logical_not(receives))
                def _():
                    frecv[d, g, k, j] = pf[g, k, j].astype(BF16)

                part(k, g, d, j, to).start()
                return 0

            lax.fori_loop(0, hi - lo, one, 0)

    lag = jnp.maximum(c, nc - 1 - c)

    def turn(k, tau):
        @pl.when(tau < groups)
        def _():
            for t in range(steps):
                lf_copy(k, tau, t).wait()
            slot = lax.rem(tau, SLOTS)
            acc = sum(dot_t(st[t, k], lf[k, slot, t].reshape(gs * 128, width)) for t in range(steps))
            pf[tau, k] = -acc.reshape(nc, hc, gs * 128)

            @pl.when(tau + SLOTS < groups)
            def _():
                for t in range(steps):
                    lf_copy(k, tau + SLOTS, t).start()

        pass_on(k, tau - c, 0, has_left, c + 1, nc, right)
        pass_on(k, tau - (nc - 1 - c), 1, has_right, 0, c, left)
        g = tau - lag

        @pl.when((g >= 0) & (g < groups))
        def _():
            @pl.when(has_left)
            def _():
                part(k, g, 0, c, right).wait_recv()
                pf[g, k, c] += frecv[0, g, k, c].astype(F32)

            @pl.when(has_right)
            def _():
                part(k, g, 1, c, left).wait_recv()
                pf[g, k, c] += frecv[1, g, k, c].astype(F32)

            for i in range(gs):
                a = steps * rounds + g * gs + i
                total = pf[g, k, c, :, i * 128 : (i + 1) * 128]
                out_rest[a, k * hc : (k + 1) * hc, :] = noise[a, k * hc : (k + 1) * hc, :] + total

    turns = groups + nc - 1
    taken = [0] * CHAINS

    def chain(k):
        for _ in range(k * LAG):
            yield
        yield from gather(k)
        for s in range(steps):
            inverse(s, k)
            yield from rowsum(s, k)
            if s < steps - 1:
                yield from colsum(s + 1, k)
        over.add(k)
        while len(over) < CHAINS and taken[k] < turns:
            turn(k, jnp.int32(taken[k]))
            taken[k] += 1
            yield

    over = set()
    live = [chain(k) for k in range(CHAINS)]
    while live:
        for one in list(live):
            if next(one, live) is live:
                live.remove(one)

    out_rest[0:rounds] = noise[0:rounds]
    owners = max(1, 128 // hl)
    units = steps * (nc // owners)
    count = turns - min(taken)
    per = -(-units // count)

    def turn_over(u):
        @pl.when(u < units)
        def _():
            s = u // (nc // owners)
            v = u % (nc // owners)
            blocks = [
                st[s, k, pl.ds(pl.multiple_of((v * owners + o) * hc, 16), hc), :]
                for o in range(owners)
                for k in range(CHAINS)
            ]
            tile = jnp.concatenate(blocks, axis=0).astype(F32)
            out_solved[s, :, pl.ds(pl.multiple_of(v * 128, 128), 128)] = tile.T.astype(BF16)

    def both(i, _):
        for k in range(CHAINS):
            turn(k, taken[k] + i)
        for p in range(per):
            turn_over(i * per + p)
        return 0

    lax.fori_loop(0, count, both, 0)

    def finish(g, _):
        def sent(k, d, to):
            def one(j, _):
                part(k, g, d, j, to).wait_send()
                return 0

            return one

        for k in range(CHAINS):
            lax.fori_loop(c + 1, nc, sent(k, 0, right), 0)
            lax.fori_loop(0, c, sent(k, 1, left), 0)
        return 0

    lax.fori_loop(0, groups, finish, 0)


def local(nr, nc, noise, factor, dinv):
    hl, rblk, rb = noise.shape
    steps, width, rounds, _ = dinv.shape
    below = factor.shape[0] - (steps - 1) * rounds
    gs = next(x for x in (3, 2, 1) if below % x == 0)
    groups = below // gs
    hc = hl // CHAINS
    rows = nc * hc
    bits = nr.bit_length() - 1
    vm = pltpu.VMEM
    dma = pltpu.SemaphoreType.DMA
    npairs = steps * (steps - 1) // 2
    solved, rest = pl.pallas_call(
        functools.partial(kernel, nr, nc),
        out_shape=(
            jax.ShapeDtypeStruct((steps, width, nc * hl), BF16),
            jax.ShapeDtypeStruct((rblk, hl, rb), F32),
        ),
        in_specs=[
            pl.BlockSpec(memory_space=pltpu.VMEM),
            pl.BlockSpec(memory_space=pl.ANY),
            pl.BlockSpec(memory_space=pl.ANY),
        ],
        out_specs=(pl.BlockSpec(memory_space=pltpu.VMEM), pl.BlockSpec(memory_space=pltpu.VMEM)),
        scratch_shapes=[
            vm((steps, rounds, width, rb), BF16),
            vm((npairs, rounds, rb, width), BF16),
            vm((CHAINS, SLOTS, steps, gs, rb, width), BF16),
            vm((steps, CHAINS, rows, width), BF16),
            vm((CHAINS, rounds, rows, rb), BF16),
            vm((CHAINS, rows, width), F32),
            vm((CHAINS, rows, width), BF16),
            vm((steps, CHAINS, rows, width), BF16),
            vm((CHAINS, rounds, rows, rb), F32),
            vm((CHAINS, 2, rounds, rows, rb), BF16),
            vm((steps - 1, CHAINS, 2, rounds, rows, rb), BF16),
            vm((groups, CHAINS, nc, hc, gs * rb), F32),
            vm((2, groups, CHAINS, nc, hc, gs * rb), BF16),
            dma((steps,)),
            dma((npairs,)),
            dma((CHAINS, SLOTS, steps)),
            dma((CHAINS, 2, nc)),
            dma((CHAINS, 2, nc)),
            dma((steps, CHAINS, 2 * bits)),
            dma((steps, CHAINS, 2 * bits)),
            dma((steps - 1, CHAINS, 2, rounds)),
            dma((steps - 1, CHAINS, 2, rounds)),
            dma((2, groups, CHAINS, nc)),
            dma((2, groups, CHAINS, nc)),
        ],
        compiler_params=pltpu.CompilerParams(
            collective_id=0, has_side_effects=True, vmem_limit_bytes=63 * 1024 * 1024
        ),
    )(
        jnp.transpose(noise, (1, 0, 2)),
        jnp.transpose(factor, (0, 2, 1, 3)),
        jnp.transpose(dinv, (0, 2, 1, 3)),
    )
    return solved, jnp.transpose(rest, (1, 0, 2))


def solution(mesh):
    placed = (P("col", None, "row"), P(None, "row", None, "col"), P(None, "col", None, "row"))
    return jax.shard_map(
        functools.partial(local, mesh.shape["row"], mesh.shape["col"]),
        mesh=mesh,
        in_specs=placed,
        out_specs=(P(None, "col", None), P("col", None, "row")),
        check_vma=False,
    )
```

```python
import functools

import jax
import jax.numpy as jnp
from jax import lax
from jax.experimental import pallas as pl
from jax.experimental.pallas import tpu as pltpu
from jax.sharding import PartitionSpec as P

BF16 = jnp.bfloat16
F32 = jnp.float32
CHAINS = 2
SLOTS = 2
LAG = 0
QB = 256


def dot_t(a, b):
    return lax.dot_general(a, b, (((1,), (1,)), ((), ())), preferred_element_type=F32)


def remote(src, dst, send_sem, recv_sem, axis, index):
    return pltpu.make_async_remote_copy(
        src_ref=src,
        dst_ref=dst,
        send_sem=send_sem,
        recv_sem=recv_sem,
        device_id={axis: index},
        device_id_type=pl.DeviceIdType.MESH,
    )


def kernel(
    nr, nc, noise, factor, dinv, out_solved, out_rest,
    dv, lp, lf, st, cur, wsum, rsend, rrecv, pz, zsend, zrecv, pf, frecv,
    dv_sem, lp_sem, lf_sem,
    g_ss, g_rs, r_ss, r_rs, z_ss, z_rs, f_ss, f_rs,
):
    steps, rounds, width = dv.shape[0], dv.shape[1], dv.shape[2]
    hl = noise.shape[1]
    hc = hl // CHAINS
    rows = nc * hc
    groups, gs = pf.shape[0], lf.shape[3]
    bits = nr.bit_length() - 1
    first = (steps - 1) * rounds
    r = lax.axis_index("row")
    c = lax.axis_index("col")
    right = jnp.minimum(c + 1, nc - 1)
    left = jnp.maximum(c - 1, 0)
    has_left = c > 0
    has_right = c < nc - 1

    def partner(b):
        return r + (1 - 2 * ((r // (1 << b)) % 2)) * (1 << b)

    dv_copy = [pltpu.make_async_copy(dinv.at[s], dv.at[s], dv_sem.at[s]) for s in range(steps)]
    pairs = [(s, t) for s in range(1, steps) for t in range(s)]
    lp_copy = [
        pltpu.make_async_copy(factor.at[pl.ds((s - 1) * rounds, rounds), t], lp.at[i], lp_sem.at[i])
        for i, (s, t) in enumerate(pairs)
    ]

    def lf_copy(k, group, t):
        slot = lax.rem(group, SLOTS)
        return pltpu.make_async_copy(
            factor.at[pl.ds(first + group * gs, gs), t], lf.at[k, slot, t], lf_sem.at[k, slot, t]
        )

    for copy in dv_copy + lp_copy:
        copy.start()
    for k in range(CHAINS):
        for group in range(min(SLOTS, groups)):
            for t in range(steps):
                lf_copy(k, jnp.int32(group), t).start()

    barrier = pltpu.get_barrier_semaphore()
    for b in range(bits):
        pl.semaphore_signal(
            barrier, inc=1, device_id={"row": partner(b)}, device_id_type=pl.DeviceIdType.MESH
        )

    @pl.when(has_left)
    def _():
        pl.semaphore_signal(barrier, inc=1, device_id={"col": left}, device_id_type=pl.DeviceIdType.MESH)

    @pl.when(has_right)
    def _():
        pl.semaphore_signal(barrier, inc=1, device_id={"col": right}, device_id_type=pl.DeviceIdType.MESH)

    pl.semaphore_wait(barrier, bits + has_left.astype(jnp.int32) + has_right.astype(jnp.int32))

    ready = set()

    def need(key, copy):
        if key not in ready:
            ready.add(key)
            copy.wait()

    def own_rows():
        return pl.ds(pl.multiple_of(c * hc, 16), hc)

    def gather(k):
        cur[k, :, own_rows(), :] = noise[0:rounds, k * hc : (k + 1) * hc, :].astype(BF16)

        def chunk(j, d, t, to):
            ref = cur.at[k, :, pl.ds(pl.multiple_of(j * hc, 16), hc), :]
            return remote(ref, ref, g_ss.at[k, d, t], g_rs.at[k, d, t], "col", to)

        for t in range(nc - 1):

            @pl.when(has_right & (c >= t))
            def _():
                chunk(c - t, 0, t, right).start()

            @pl.when(has_left & (c + t < nc))
            def _():
                chunk(c + t, 1, t, left).start()

            yield

            @pl.when(c - 1 - t >= 0)
            def _():
                chunk(c - 1 - t, 0, t, right).wait_recv()

            @pl.when(c + 1 + t < nc)
            def _():
                chunk(c + 1 + t, 1, t, left).wait_recv()

        for t in range(nc - 1):

            @pl.when(has_right & (c >= t))
            def _():
                chunk(c - t, 0, t, right).wait_send()

            @pl.when(has_left & (c + t < nc))
            def _():
                chunk(c + t, 1, t, left).wait_send()

    def inverse(s, k):
        need(("dv", s), dv_copy[s])
        lhs = jnp.concatenate([cur[k, d] for d in range(rounds)], axis=-1)

        @pl.loop(0, width // QB)
        def _(i):
            q = pl.ds(pl.multiple_of(i * QB, QB), QB)
            rhs = jnp.concatenate([dv[s, d, q, :] for d in range(rounds)], axis=-1)
            wsum[k, :, q] = dot_t(lhs, rhs)

    def rowsum(s, k):
        order = list(range(bits))
        if k % 2 == 1:
            order = order[:1] + order[1:][::-1]
        base = jnp.int32(0)
        size = rows
        place = 0
        for i, b in enumerate(order):
            half = size // 2
            bit = (r // (1 << b)) % 2
            keep = pl.multiple_of(base + bit * half, 16)
            away = pl.multiple_of(base + (1 - bit) * half, 16)
            area = pl.ds(place, half)
            rsend[k, area, :] = wsum[k, pl.ds(away, half), :].astype(BF16)
            copy = remote(
                rsend.at[k, area], rrecv.at[s, k, area], r_ss.at[s, k, i], r_rs.at[s, k, i], "row", partner(b)
            )
            copy.start()
            yield
            copy.wait_recv()
            total = wsum[k, pl.ds(keep, half), :] + rrecv[s, k, area, :].astype(F32)
            if i < bits - 1:
                wsum[k, pl.ds(keep, half), :] = total
            else:
                st[s, k, pl.ds(keep, half), :] = total.astype(BF16)
            copy.wait_send()
            base, size = keep, half
            place += half
        for i, b in reversed(list(enumerate(order))):
            bit = (r // (1 << b)) % 2
            mine = st.at[s, k, pl.ds(pl.multiple_of(base, 16), size)]
            j = bits + i
            copy = remote(mine, mine, r_ss.at[s, k, j], r_rs.at[s, k, j], "row", partner(b))
            copy.start()
            yield
            copy.wait()
            base = base - bit * size
            size = size * 2

    def colsum(s, k):
        mine = [(i, t) for i, (s_, t) in enumerate(pairs) if s_ == s]
        for i, _ in mine:
            need(("lp", i), lp_copy[i])

        update = sum(dot_t(st[t, k], lp[i].reshape(rounds * 128, width)) for i, t in mine)
        for a in range(rounds):
            pz[k, a] = -update[:, a * 128 : (a + 1) * 128]

        @pl.loop(0, rounds)
        def _(a):
            pz[k, a, own_rows(), :] += noise[s * rounds + a, k * hc : (k + 1) * hc, :]

        def message(a, d, to):
            return remote(
                zsend.at[k, d, a], zrecv.at[s - 1, k, d, a], z_ss.at[s - 1, k, d, a], z_rs.at[s - 1, k, d, a], "col", to
            )

        def move(a, d, receives, sends, to):
            @pl.when((a >= 0) & (a < rounds))
            def _():
                @pl.when(receives)
                def _():
                    message(a, d, to).wait_recv()

                @pl.when(sends & receives)
                def _():
                    zsend[k, d, a] = (pz[k, a] + zrecv[s - 1, k, d, a].astype(F32)).astype(BF16)

                @pl.when(sends & jnp.logical_not(receives))
                def _():
                    zsend[k, d, a] = pz[k, a].astype(BF16)

                @pl.when(sends)
                def _():
                    message(a, d, to).start()

        for tau in range(rounds + nc - 1):
            move(tau - c, 0, has_left, has_right, right)
            move(tau - (nc - 1 - c), 1, has_right, has_left, left)
            yield

        @pl.loop(0, rounds)
        def _(a):
            @pl.when(has_left)
            def _():
                pz[k, a] += zrecv[s - 1, k, 0, a].astype(F32)

            @pl.when(has_right)
            def _():
                pz[k, a] += zrecv[s - 1, k, 1, a].astype(F32)

            cur[k, a] = pz[k, a].astype(BF16)
            out_rest[s * rounds + a, k * hc : (k + 1) * hc, :] = pz[k, a, own_rows(), :]

            @pl.when(has_right)
            def _():
                message(a, 0, right).wait_send()

            @pl.when(has_left)
            def _():
                message(a, 1, left).wait_send()

    def part(k, g, d, j, to):
        ref = frecv.at[d, g, k, j]
        return remote(ref, ref, f_ss.at[d, g, k, j], f_rs.at[d, g, k, j], "col", to)

    def pass_on(k, g, d, receives, lo, hi, to):
        @pl.when((g >= 0) & (g < groups))
        def _():
            def one(i, _):
                j = (hi - 1 - i) if d == 0 else (lo + i)

                @pl.when(receives)
                def _():
                    part(k, g, d, j, to).wait_recv()
                    frecv[d, g, k, j] = (pf[g, k, j] + frecv[d, g, k, j].astype(F32)).astype(BF16)

                @pl.when(jnp.logical_not(receives))
                def _():
                    frecv[d, g, k, j] = pf[g, k, j].astype(BF16)

                part(k, g, d, j, to).start()
                return 0

            lax.fori_loop(0, hi - lo, one, 0)

    lag = jnp.maximum(c, nc - 1 - c)

    def turn(k, tau):
        @pl.when(tau < groups)
        def _():
            for t in range(steps):
                lf_copy(k, tau, t).wait()
            slot = lax.rem(tau, SLOTS)
            acc = sum(dot_t(st[t, k], lf[k, slot, t].reshape(gs * 128, width)) for t in range(steps))
            pf[tau, k] = -acc.reshape(nc, hc, gs * 128)

            @pl.when(tau + SLOTS < groups)
            def _():
                for t in range(steps):
                    lf_copy(k, tau + SLOTS, t).start()

        pass_on(k, tau - c, 0, has_left, c + 1, nc, right)
        pass_on(k, tau - (nc - 1 - c), 1, has_right, 0, c, left)
        g = tau - lag

        @pl.when((g >= 0) & (g < groups))
        def _():
            @pl.when(has_left)
            def _():
                part(k, g, 0, c, right).wait_recv()
                pf[g, k, c] += frecv[0, g, k, c].astype(F32)

            @pl.when(has_right)
            def _():
                part(k, g, 1, c, left).wait_recv()
                pf[g, k, c] += frecv[1, g, k, c].astype(F32)

            for i in range(gs):
                a = steps * rounds + g * gs + i
                total = pf[g, k, c, :, i * 128 : (i + 1) * 128]
                out_rest[a, k * hc : (k + 1) * hc, :] = noise[a, k * hc : (k + 1) * hc, :] + total

    turns = groups + nc - 1
    taken = [0] * CHAINS

    def chain(k):
        for _ in range(k * LAG):
            yield
        yield from gather(k)
        for s in range(steps):
            inverse(s, k)
            yield from rowsum(s, k)
            if s < steps - 1:
                yield from colsum(s + 1, k)
        over.add(k)
        while len(over) < CHAINS and taken[k] < turns:
            turn(k, jnp.int32(taken[k]))
            taken[k] += 1
            yield

    over = set()
    live = [chain(k) for k in range(CHAINS)]
    while live:
        for one in list(live):
            if next(one, live) is live:
                live.remove(one)

    out_rest[0:rounds] = noise[0:rounds]
    owners = max(1, 128 // hl)
    units = steps * (nc // owners)
    count = turns - min(taken)
    per = -(-units // count)

    def turn_over(u):
        @pl.when(u < units)
        def _():
            s = u // (nc // owners)
            v = u % (nc // owners)
            blocks = [
                st[s, k, pl.ds(pl.multiple_of((v * owners + o) * hc, 16), hc), :]
                for o in range(owners)
                for k in range(CHAINS)
            ]
            tile = jnp.concatenate(blocks, axis=0).astype(F32)
            out_solved[s, :, pl.ds(pl.multiple_of(v * 128, 128), 128)] = tile.T.astype(BF16)

    def both(i, _):
        for k in range(CHAINS):
            turn(k, taken[k] + i)
        for p in range(per):
            turn_over(i * per + p)
        return 0

    lax.fori_loop(0, count, both, 0)

    def finish(g, _):
        def sent(k, d, to):
            def one(j, _):
                part(k, g, d, j, to).wait_send()
                return 0

            return one

        for k in range(CHAINS):
            lax.fori_loop(c + 1, nc, sent(k, 0, right), 0)
            lax.fori_loop(0, c, sent(k, 1, left), 0)
        return 0

    lax.fori_loop(0, groups, finish, 0)


def local(nr, nc, noise, factor, dinv):
    hl, rblk, rb = noise.shape
    steps, width, rounds, _ = dinv.shape
    below = factor.shape[0] - (steps - 1) * rounds
    gs = next(x for x in (3, 2, 1) if below % x == 0)
    groups = below // gs
    hc = hl // CHAINS
    rows = nc * hc
    bits = nr.bit_length() - 1
    vm = pltpu.VMEM
    dma = pltpu.SemaphoreType.DMA
    npairs = steps * (steps - 1) // 2
    solved, rest = pl.pallas_call(
        functools.partial(kernel, nr, nc),
        out_shape=(
            jax.ShapeDtypeStruct((steps, width, nc * hl), BF16),
            jax.ShapeDtypeStruct((rblk, hl, rb), F32),
        ),
        in_specs=[
            pl.BlockSpec(memory_space=pltpu.VMEM),
            pl.BlockSpec(memory_space=pl.ANY),
            pl.BlockSpec(memory_space=pl.ANY),
        ],
        out_specs=(pl.BlockSpec(memory_space=pltpu.VMEM), pl.BlockSpec(memory_space=pltpu.VMEM)),
        scratch_shapes=[
            vm((steps, rounds, width, rb), BF16),
            vm((npairs, rounds, rb, width), BF16),
            vm((CHAINS, SLOTS, steps, gs, rb, width), BF16),
            vm((steps, CHAINS, rows, width), BF16),
            vm((CHAINS, rounds, rows, rb), BF16),
            vm((CHAINS, rows, width), F32),
            vm((CHAINS, rows, width), BF16),
            vm((steps, CHAINS, rows, width), BF16),
            vm((CHAINS, rounds, rows, rb), F32),
            vm((CHAINS, 2, rounds, rows, rb), BF16),
            vm((steps - 1, CHAINS, 2, rounds, rows, rb), BF16),
            vm((groups, CHAINS, nc, hc, gs * rb), F32),
            vm((2, groups, CHAINS, nc, hc, gs * rb), BF16),
            dma((steps,)),
            dma((npairs,)),
            dma((CHAINS, SLOTS, steps)),
            dma((CHAINS, 2, nc)),
            dma((CHAINS, 2, nc)),
            dma((steps, CHAINS, 2 * bits)),
            dma((steps, CHAINS, 2 * bits)),
            dma((steps - 1, CHAINS, 2, rounds)),
            dma((steps - 1, CHAINS, 2, rounds)),
            dma((2, groups, CHAINS, nc)),
            dma((2, groups, CHAINS, nc)),
        ],
        compiler_params=pltpu.CompilerParams(
            collective_id=0, has_side_effects=True, vmem_limit_bytes=63 * 1024 * 1024
        ),
    )(
        jnp.transpose(noise, (1, 0, 2)),
        jnp.transpose(factor, (0, 2, 1, 3)),
        jnp.transpose(dinv, (0, 2, 1, 3)),
    )
    return solved, jnp.transpose(rest, (1, 0, 2))


def solution(mesh):
    placed = (P("col", None, "row"), P(None, "row", None, "col"), P(None, "col", None, "row"))
    return jax.shard_map(
        functools.partial(local, mesh.shape["row"], mesh.shape["col"]),
        mesh=mesh,
        in_specs=placed,
        out_specs=(P(None, "col", None), P("col", None, "row")),
        check_vma=False,
    )
```
